512 devices in a mesh: seq: 32 (over x, z_hi, core), fsdp: 16 (over z_lo, y).
Axes of the slice: x: 4, y: 8, z: 8 (z_hi: 4, z_lo: 2; z = z_hi * 2 + z_lo), core: 2. Of those that a mesh axis runs over, the one named last changes fastest.
Arguments:
- hidden: bfloat16 [16, 4096, 5120], P('fsdp', 'seq'), may hold values from -6 to 6
- step_index: int32 [16], P('fsdp'), may hold values from 0 to 3
- block_sizes: int32 [16, 6], P('fsdp'), may hold values from 1 to 3, 16 in all within a row
- teacher_mod: float32 [4, 2, 5120], P(None, None, 'fsdp'), may hold values from -3 to 3
- critic_mod: float32 [4, 2, 5120], P(None, None, 'fsdp'), may hold values from -3 to 3
- teacher_weights: bfloat16 [3, 5120, 128], P(None, 'fsdp'), may hold values from -0.16699219 to 0.16699219
- critic_weights: bfloat16 [3, 5120, 128], P(None, 'fsdp'), may hold values from -0.16699219 to 0.16699219
Outputs:
- score_gap: float32 [16, 4096, 128], P('fsdp', 'seq')
The draws below stay inside these ranges and needn't reach their ends.
Inputs may be any that keep to these rules, and one draw needn't show every extreme that they name: `block_sizes`: each clip's frame counts sum to 16, and some block of every clip holds exactly 3 frames.
All inputs are finite; a program needn't handle non-finite values.
Results may differ from the reference program's by a relative error of at most 0.012.
The reference program's roundings to bfloat16 on the way count: a program that leaves them out, or rounds other values in their place, can miss the bound.
Values may be sent and summed in bfloat16 or wider, within the bound.
A program may use at most 64 MiB of HBM per device.

```python
import math
import jax
import jax.numpy as jnp
import numpy as np
from jax import lax

D = 5120
HD = 128
TOK_DEV = 128
NSTEPS = 4
FRAMES = 16
NBLK = 6
L = 4096
FRAME_TOK = 256
CLIPS = 16


def set_ends(array, rng, least, largest):
    longest = array.shape.index(max(array.shape))
    spots = []
    for shift in (0, 1):
        where = [jax.random.randint(jax.random.fold_in(rng, axis), (), 0, length) for axis, length in enumerate(array.shape)]
        where[longest] = (where[longest] + shift) % array.shape[longest]
        spots.append(tuple(where))
    return array.at[spots[0]].set(least).at[spots[1]].set(largest)


def steps_of(own_key, shape, shards, least, top_value):
    def one(axis_at, blocks):
        draws = jax.random.uniform(jax.random.fold_in(jax.random.fold_in(own_key, 6), axis_at), (blocks,), jnp.float32, least / len(shards), top_value / len(shards))
        return jnp.repeat(jnp.exp(draws), shape[axis_at] // blocks).reshape((-1,) + (1,) * (len(shape) - axis_at - 1))

    factor_of = one(*shards[0])
    for cut in shards[1:]:
        factor_of = factor_of * one(*cut)
    return factor_of


def split_up(number_of, total, limit, slope):
    portions = [(1 << 20) // math.isqrt(standing ** slope) + 1 for standing in range(2, number_of + 1)]
    surplus, counts = total - limit - (number_of - 1), [1] * (number_of - 1)
    while surplus > 0:
        free = [i for i in range(number_of - 1) if counts[i] < limit]
        whole, left = sum([portions[i] for i in free]), surplus
        for i in free:
            more = min(limit - counts[i], max(1, left * portions[i] // whole), surplus)
            counts[i] = counts[i] + more
            surplus = surplus - more
    return np.array([limit] + counts)


def uneven_parts(stream_key, number_of, total, reach, skew):
    if number_of == 2:
        one = jax.random.randint(stream_key, (), max(1, total - reach), min(reach, total - 1) + 1)
        return jnp.stack([one, total - one])
    lengths = jnp.asarray(split_up(number_of, total, reach, skew), jnp.int32)
    pairs = (number_of - 1) // 2
    giver, taker = lengths[1:1 + 2 * pairs:2], lengths[2:2 + 2 * pairs:2]
    margin = jnp.minimum(giver - 1, reach - taker)
    moved = jax.random.randint(jax.random.fold_in(stream_key, 1), (pairs,), 0, 1 << 20) % (margin + 1)
    lengths = lengths.at[1:1 + 2 * pairs:2].set(giver - moved).at[2:2 + 2 * pairs:2].set(taker + moved)
    return lengths[jax.random.permutation(jax.random.fold_in(stream_key, 2), number_of)]


def normal_values(stream_key, extent, deviation, bound, cuts=(), kind=jnp.bfloat16):
    drawn = jax.random.normal(stream_key, extent, jnp.float32) * deviation
    if len(cuts) > 0:
        drawn = steps_of(stream_key, extent, cuts, -0.22, 0.18) * drawn
    return jnp.clip(drawn, min=-bound, max=bound).astype(kind)


def setup_inputs(seed: int = 0) -> dict:
    splits = jax.random.split(jax.random.key(seed), 8)
    hidden = normal_values(splits[0], (CLIPS, L, D), 1.0, 6.0, ((0, 16), (1, 32)))
    step_index = set_ends(jax.random.randint(splits[1], (CLIPS,), 0, NSTEPS), jax.random.fold_in(splits[1], 1), 0, NSTEPS - 1).astype(jnp.int32)
    block_sizes = jax.vmap(lambda own: uneven_parts(own, NBLK, FRAMES, 3, 1))(jax.random.split(splits[2], CLIPS)).reshape((CLIPS, NBLK)).astype(jnp.int32)
    teacher_mod = normal_values(splits[3], (NSTEPS, 2, D), 0.5, 3.0, ((2, 16),), jnp.float32)
    critic_mod = normal_values(splits[4], (NSTEPS, 2, D), 0.5, 3.0, ((2, 16),), jnp.float32)
    teacher_weights = normal_values(splits[5], (3, D, HD), (2 * D ** -0.5), 0.16699219, ((1, 16),))
    critic_weights = normal_values(splits[6], (3, D, HD), (2 * D ** -0.5), 0.16699219, ((1, 16),))
    return {"hidden": hidden, "step_index": step_index, "block_sizes": block_sizes, "teacher_mod": teacher_mod, "critic_mod": critic_mod, "teacher_weights": teacher_weights, "critic_weights": critic_weights}


def head_output(normed, step, blocks, mod, weights):
    pick = (jnp.arange(NSTEPS, dtype=jnp.int32) == step)[:, None]
    shift = lax.optimization_barrier(jnp.sum(jnp.where(pick, mod[:, 0, :], jnp.float32(0.0)), axis=0))
    scale = lax.optimization_barrier(jnp.sum(jnp.where(pick, mod[:, 1, :], jnp.float32(0.0)), axis=0))
    x_mod = (normed * (1.0 + scale) + shift).astype(jnp.bfloat16)
    query = jnp.dot(x_mod, weights[0], preferred_element_type=jnp.float32).astype(jnp.bfloat16)
    keys = jnp.dot(x_mod, weights[1], preferred_element_type=jnp.float32).astype(jnp.bfloat16)
    values = jnp.dot(x_mod, weights[2], preferred_element_type=jnp.float32).astype(jnp.bfloat16)

    def one_block(index):
        start = (index * TOK_DEV).astype(jnp.int32)
        rows_q = lax.dynamic_slice_in_dim(query, start, TOK_DEV, 0)
        rows_b = lax.dynamic_slice_in_dim(blocks, start, TOK_DEV, 0)
        scores = jnp.dot(rows_q, keys.T, preferred_element_type=jnp.float32) / jnp.sqrt(jnp.float32(HD))
        visible = blocks[None, :] <= rows_b[:, None]
        scores = jnp.where(visible, scores, -jnp.inf)
        top = lax.optimization_barrier(jnp.max(scores, axis=1, keepdims=True))
        expo = jnp.where(visible, jnp.exp(scores - top), jnp.float32(0.0))
        denom = lax.optimization_barrier(jnp.sum(expo, axis=1, keepdims=True))
        return jnp.dot(expo.astype(jnp.bfloat16), values, preferred_element_type=jnp.float32) / denom
    outs = lax.map(one_block, jnp.arange(L // TOK_DEV, dtype=jnp.int32))
    return outs.reshape(L, HD)

def reference(hidden, step_index, block_sizes, teacher_mod, critic_mod, teacher_weights, critic_weights):

    def one_clip(items):
        rows, step, sizes = items
        wide = rows.astype(jnp.float32)
        mean = lax.optimization_barrier(jnp.mean(wide, axis=1, keepdims=True))
        var = lax.optimization_barrier(jnp.mean((wide - mean) ** 2, axis=1, keepdims=True))
        normed = (wide - mean) / jnp.sqrt(var + 1e-06)
        ends = (jnp.cumsum(sizes) * FRAME_TOK).astype(jnp.int32)
        places = jnp.arange(L, dtype=jnp.int32)
        blocks = lax.optimization_barrier(jnp.sum((ends[None, :] <= places[:, None]).astype(jnp.int32), axis=1)).astype(jnp.int32)
        teacher_out = head_output(normed, step, blocks, teacher_mod, teacher_weights)
        critic_out = head_output(normed, step, blocks, critic_mod, critic_weights)
        return critic_out - teacher_out
    return lax.map(one_clip, (hidden, step_index, block_sizes))
```

```python
import jax
import jax.numpy as jnp
from jax import lax
from jax.experimental import pallas as pl
from jax.experimental.pallas import tpu as pltpu
from jax.sharding import PartitionSpec as P

MESH = pl.DeviceIdType.MESH
NX, NY, NZ = 4, 8, 8
D, HD, TOK = 5120, 128, 128
SH = D // 16
QR = SH // NX
STEPS, BLKS = 4, 6
FT = 2 * TOK
HIDE = -1e30
QUERY, KEY, VALUE = 0, 1, 2
F32, BF16 = jnp.float32, jnp.bfloat16
RING = {0: (0,), 1: (-1, 1), 2: (-2, 2), 3: (-3, 3), 4: (4,)}
Z_UP = (0, -1, 2, -3)


def device(x, y, z, core):
    x, y, z = lax.rem(x + NX, NX), lax.rem(y + NY, NY), lax.rem(z + NZ, NZ)
    return ((x * 4 + lax.div(z, 2)) * 2 + core, lax.rem(z, 2) * NY + y)


def kernel(
    hid, step_ref, sizes_ref, tmod, cmod, tw, cw, out,
    H, N, X, W, T, ACC, KB, VT, QB, OA, ML, OS, OR, MR, FX,
    loc, hsem, ys, yr, zs, zr, xs, xr, as_, ar, bs, br, os_, or_, fsem,
):
    seq, fsdp = lax.axis_index("seq"), lax.axis_index("fsdp")
    core, zh, x = lax.rem(seq, 2), lax.rem(lax.div(seq, 2), 4), lax.div(seq, 8)
    y, zl = lax.rem(fsdp, NY), lax.div(fsdp, NY)
    z = zh * 2 + zl
    up, down = device(x, y + 1, z, core), device(x, y - 1, z, core)
    zup, zdown = device(x, y, z + 1, core), device(x, y, z - 1, core)
    zup2, zdown2 = device(x, y, z + 2, core), device(x, y, z - 2, core)
    xup, xdown, xfar = (device(x + k, y, z, core) for k in (1, -1, 2))
    other = device(x, y, z, 1 - core)
    peers = (up, down, zup, zdown, zup2, zdown2, xup, xdown, xfar, other)

    def shard(par, delta):
        side = zl if par == 0 else 1 - zl
        return side * NY + lax.rem(y + delta + NY, NY)

    own = shard(0, 0)
    started = []

    def send(src, dst, ssem, rsem, to):
        copy = pltpu.make_async_remote_copy(
            src_ref=src, dst_ref=dst, send_sem=ssem, recv_sem=rsem, device_id=to, device_id_type=MESH
        )
        copy.start()
        started.append(copy)

    def arrived(ref, rsem):
        pltpu.make_async_remote_copy(
            src_ref=ref, dst_ref=ref, send_sem=rsem, recv_sem=rsem, device_id=other, device_id_type=MESH
        ).wait_recv()

    take_h = pltpu.make_async_copy(hid.at[0], H.at[0], loc.at[0])
    take_h.start()

    @pl.when(core == 0)
    def _():
        pltpu.make_async_copy(tw, W.at[own], loc.at[1]).start()
        pltpu.make_async_copy(tmod, T.at[own], loc.at[2]).start()

    @pl.when(core == 1)
    def _():
        pltpu.make_async_copy(cw, W.at[own], loc.at[1]).start()
        pltpu.make_async_copy(cmod, T.at[own], loc.at[2]).start()

    barrier = pltpu.get_barrier_semaphore()
    for peer in peers:
        pl.semaphore_signal(barrier, inc=1, device_id=peer, device_id_type=MESH)
    pltpu.make_async_copy(tw, W.at[own], loc.at[1]).wait()
    pltpu.make_async_copy(tmod, T.at[own], loc.at[2]).wait()
    pl.semaphore_wait(barrier, len(peers))

    def quarter(d, k):
        return W.at[d, QUERY, pl.ds(pl.multiple_of(lax.rem(x + k + NX, NX) * QR, 16), QR)]

    def piece(what, d):
        if what == "q":
            return quarter(d, 0)
        if what == "t":
            return T.at[d]
        return W.at[d, KEY if what == "k" else VALUE]

    kinds = ("q", "t", "k", "v")
    ysems, zsems, xsems = {}, {}, {}

    def ysem(what, delta):
        return ysems.setdefault((what, delta), len(ysems))

    def zsem(what, delta):
        return zsems.setdefault((what, delta), len(zsems))

    def xsem(par, delta, k):
        return xsems.setdefault((par, delta, k), len(xsems))

    def ysend(what, delta, to):
        there = delta - to
        if there == -4:
            there = 4
        i = ysem(what, there)
        ref = piece(what, shard(0, delta))
        send(ref, ref, ys.at[i], yr.at[i], up if to == 1 else down)

    def zsend(what, delta):
        if what == "q":
            to = zup if delta in Z_UP else zdown
        else:
            to = zdown if what == "v" else zup
        i = zsem(what, delta)
        ref = piece(what, shard(0, delta))
        send(ref, ref, zs.at[i], zr.at[i], to)

    def xsend(par, delta, far=0):
        d = shard(par, delta)
        for k in (1, -1) if far == 0 else (far,):
            there = -k if far == 0 else 2
            i = xsem(par, delta, there)
            ref = quarter(d, 0 if far == 0 else -far)
            send(ref, ref, xs.at[i], xr.at[i], xup if k == 1 else xdown)

    def y_step(s):
        for what in kinds:
            for delta in RING[s]:
                if s > 0:
                    arrived(piece(what, shard(0, delta)), yr.at[ysem(what, delta)])
                d_ = delta
                if s == 0:
                    ysend(what, 0, 1)
                    ysend(what, 0, -1)
                elif s < 3:
                    ysend(what, d_, 1 if d_ < 0 else -1)
                elif s == 3 and (d_ > 0) == (what == "v"):
                    ysend(what, d_, 1 if d_ < 0 else -1)
                zsend(what, d_)
                if what == "q" and s > 0:
                    xsend(0, d_)

    def zq(s):
        for delta in RING[s]:
            arrived(piece("q", shard(1, delta)), zr.at[zsem("q", delta)])
            xsend(1, delta)

    def x_near(par, s):
        for delta in RING[s]:
            d = shard(par, delta)
            arrived(quarter(d, -1), xr.at[xsem(par, delta, -1)])
            if par == 0:
                xsend(par, delta, 1)
            arrived(quarter(d, 1), xr.at[xsem(par, delta, 1)])
            if par == 1:
                xsend(par, delta, -1)

    def x_far(par, s):
        for delta in RING[s]:
            arrived(quarter(shard(par, delta), 2), xr.at[xsem(par, delta, 2)])

    def norm_rows(slot):
        def body(i, carry):
            rows = pl.ds(pl.multiple_of(i * 16, 16), 16)
            wide = H[slot, rows, :].astype(F32)
            mean = jnp.sum(wide, axis=1, keepdims=True) * F32(1.0 / D)
            dev = wide - mean
            var = jnp.sum(dev * dev, axis=1, keepdims=True) * F32(1.0 / D)
            normed = dev * (F32(1.0) / jnp.sqrt(var + F32(1e-6)))
            there = pl.ds(pl.multiple_of(slot * TOK + i * 16, 16), 16)
            for d in range(16):
                N[d, there, :] = normed[:, d * SH : (d + 1) * SH]
            return carry

        lax.fori_loop(0, TOK // 16, body, 0)

    ACC[...] = jnp.zeros_like(ACC)
    step = step_ref[0]

    def project(par, s):
        def one(d):
            shift, scale = T[d, 0, 0:1, :], T[d, 0, 1:2, :]
            for k in range(1, STEPS):
                shift = jnp.where(step == k, T[d, k, 0:1, :], shift)
                scale = jnp.where(step == k, T[d, k, 1:2, :], scale)
            mod = (N[d] * (F32(1.0) + scale) + shift).astype(BF16)
            X[d] = mod
            ACC[KEY] += jnp.dot(mod, W[d, KEY], preferred_element_type=F32)
            ACC[VALUE] += jnp.dot(mod, W[d, VALUE], preferred_element_type=F32)

        if len(RING[s]) == 1:
            one(shard(par, RING[s][0]))
        else:

            def body(i, carry):
                one(shard(par, s * (2 * i - 1)))
                return carry

            lax.fori_loop(0, 2, body, 0)

    def z_step(s):
        for delta in RING[s]:
            for what in ("t", "k", "v"):
                arrived(piece(what, shard(1, delta)), zr.at[zsem(what, delta)])
        project(1, s)

    y_step(0)
    send(hid.at[0], H.at[1], hsem.at[0], hsem.at[1], other)
    take_h.wait()
    norm_rows(0)
    y_step(1)
    zq(0)
    arrived(H.at[1], hsem.at[1])
    norm_rows(1)
    y_step(2)
    zq(1)
    x_near(1, 0)
    x_near(0, 1)
    project(0, 0)
    project(0, 1)
    z_step(0)
    y_step(3)
    zq(2)
    x_near(1, 1)
    x_near(0, 2)
    project(0, 2)
    z_step(1)
    y_step(4)
    zq(3)
    x_near(1, 2)
    x_near(0, 3)
    project(0, 3)
    project(0, 4)
    zq(4)
    x_near(1, 3)
    x_near(0, 4)
    z_step(2)
    x_near(1, 4)
    z_step(3)
    z_step(4)

    KB[0] = ACC[KEY].astype(BF16)
    send(KB.at[0], KB.at[3], as_.at[0], ar.at[0], zup2)
    send(KB.at[0], KB.at[1], as_.at[1], ar.at[1], zdown2)
    VT[0] = ACC[VALUE].T.astype(BF16)
    send(VT.at[0], VT.at[3], as_.at[2], ar.at[2], zup2)
    send(VT.at[0], VT.at[1], as_.at[3], ar.at[3], zdown2)

    for s in range(5):
        if s > 0:
            x_far(0, s)
        x_far(1, s)

    def query(d, carry):
        ACC[QUERY] += jnp.dot(X[d], W[d, QUERY], preferred_element_type=F32)
        return carry

    lax.fori_loop(0, 16, query, 0)
    QB[0] = ACC[QUERY].astype(BF16)
    send(QB.at[0], QB.at[2], bs.at[1], br.at[1], xfar)
    send(QB.at[0], QB.at[3], bs.at[0], br.at[0], xup)
    send(QB.at[0], QB.at[1], bs.at[2], br.at[2], xdown)

    ends = []
    total = jnp.int32(0)
    for j in range(BLKS):
        total = total + sizes_ref[0, j]
        ends.append(total)

    def block_of(frame):
        number = jnp.int32(0)
        for end in ends:
            number = number + jnp.where(end <= frame, jnp.int32(1), jnp.int32(0))
        return number

    root = F32(1.0 / 128.0**0.5)

    def attend(r, slot, first):
        key_block = block_of(x * 4 + lax.rem(zh + slot, 4))
        query_block = block_of(lax.rem(x + r, NX) * 4 + zh)
        bias = jnp.where(key_block <= query_block, F32(0.0), F32(HIDE))
        s = lax.dot_general(KB[slot], QB[r], (((1,), (1,)), ((), ())), preferred_element_type=F32)
        s = s * root + bias
        top = jnp.max(s, axis=0, keepdims=True)
        if not first:
            before = ML[r, 0:1, :]
            top = jnp.maximum(top, before)
            keep = jnp.exp(before - top)
        e = jnp.exp(s - top)
        den = jnp.sum(e, axis=0, keepdims=True)
        o = jnp.dot(VT[slot], e.astype(BF16), preferred_element_type=F32)
        if not first:
            den = den + keep * ML[r, 1:2, :]
            o = o + keep * OA[r]
        ML[r, 0:1, :] = top
        ML[r, 1:2, :] = den
        OA[r] = o

    def attend_planes(slot, first=False):
        def body(r, carry):
            attend(r, slot, first)
            return carry

        lax.fori_loop(0, 4, body, 0)

    arrived(KB.at[3], ar.at[0])
    send(KB.at[3], KB.at[2], as_.at[4], ar.at[4], zup2)
    arrived(KB.at[1], ar.at[1])
    arrived(VT.at[3], ar.at[2])
    arrived(VT.at[1], ar.at[3])
    send(VT.at[1], VT.at[2], as_.at[5], ar.at[5], zdown2)
    for r in (1, 2, 3):
        arrived(QB.at[r], br.at[3 - r])
    attend_planes(0, first=True)
    attend_planes(1)
    attend_planes(3)
    arrived(KB.at[2], ar.at[4])
    arrived(VT.at[2], ar.at[5])

    for r, to in ((2, xfar), (1, xup), (3, xdown)):
        attend(r, 2, False)
        OS[r - 1] = OA[r].astype(BF16)
        send(OS.at[r - 1], OR.at[3 - r], os_.at[r - 1], or_.at[r - 1], to)
        send(ML.at[r], MR.at[3 - r], os_.at[r + 2], or_.at[r + 2], to)
    attend(0, 2, False)
    for r in (2, 1, 3):
        arrived(OR.at[3 - r], or_.at[r - 1])
        arrived(MR.at[3 - r], or_.at[r + 2])
    top = ML[0, 0:1, :]
    for i in range(3):
        top = jnp.maximum(top, MR[i, 0:1, :])
    w = jnp.exp(ML[0, 0:1, :] - top)
    den, o = w * ML[0, 1:2, :], w * OA[0]
    for i in range(3):
        w = jnp.exp(MR[i, 0:1, :] - top)
        den = den + w * MR[i, 1:2, :]
        o = o + w * OR[i].astype(F32)
    o = (o / den).T
    FX[0] = o[TOK:, :]
    send(FX.at[0], FX.at[1], fsem.at[0], fsem.at[1], other)
    arrived(FX.at[1], fsem.at[1])
    sign = jnp.where(core == 0, F32(1.0), F32(-1.0))
    out[0] = (FX[1] - o[:TOK, :]) * sign

    for copy in started:
        copy.wait_send()


def per_device(hidden, step_index, block_sizes, teacher_mod, critic_mod, teacher_weights, critic_weights):
    vmem, smem, hbm = (pl.BlockSpec(memory_space=m) for m in (pltpu.VMEM, pltpu.SMEM, pl.ANY))
    dma = pltpu.SemaphoreType.DMA
    return pl.pallas_call(
        kernel,
        out_shape=jax.ShapeDtypeStruct((1, TOK, HD), F32),
        in_specs=[hbm, smem, smem, hbm, hbm, hbm, hbm],
        out_specs=vmem,
        scratch_shapes=[
            pltpu.VMEM((2, TOK, D), BF16),
            pltpu.VMEM((16, FT, SH), F32),
            pltpu.VMEM((16, FT, SH), BF16),
            pltpu.VMEM((16, 3, SH, HD), BF16),
            pltpu.VMEM((16, STEPS, 2, SH), F32),
            pltpu.VMEM((3, FT, HD), F32),
            pltpu.VMEM((4, FT, HD), BF16),
            pltpu.VMEM((4, HD, FT), BF16),
            pltpu.VMEM((4, FT, HD), BF16),
            pltpu.VMEM((4, HD, FT), F32),
            pltpu.VMEM((4, 8, FT), F32),
            pltpu.VMEM((3, HD, FT), BF16),
            pltpu.VMEM((3, HD, FT), BF16),
            pltpu.VMEM((3, 8, FT), F32),
            pltpu.VMEM((2, TOK, HD), F32),
            dma((3,)),
            dma((2,)),
            dma((28,)),
            dma((28,)),
            dma((32,)),
            dma((32,)),
            dma((45,)),
            dma((45,)),
            dma((6,)),
            dma((6,)),
            dma((3,)),
            dma((3,)),
            dma((6,)),
            dma((6,)),
            dma((2,)),
        ],
        compiler_params=pltpu.CompilerParams(
            collective_id=0, has_side_effects=True, vmem_limit_bytes=48 * 2**20
        ),
        cost_estimate=pl.CostEstimate(flops=3 * 10**9, bytes_accessed=4 * 10**6, transcendentals=10**6),
    )(hidden, step_index, block_sizes, teacher_mod, critic_mod, teacher_weights, critic_weights)


def solution(mesh):
    return jax.shard_map(
        per_device,
        mesh=mesh,
        in_specs=(
            P("fsdp", "seq", None),
            P("fsdp"),
            P("fsdp", None),
            P(None, None, "fsdp"),
            P(None, None, "fsdp"),
            P(None, "fsdp", None),
            P(None, "fsdp", None),
        ),
        out_specs=P("fsdp", "seq", None),
        check_vma=False,
    )
```

```python
import jax
import jax.numpy as jnp
from jax import lax
from jax.experimental import pallas as pl
from jax.experimental.pallas import tpu as pltpu
from jax.sharding import PartitionSpec as P

MESH = pl.DeviceIdType.MESH
NX, NY, NZ = 4, 8, 8
D, HD, TOK = 5120, 128, 128
SH = D // 16
QR = SH // NX
STEPS, BLKS = 4, 6
QMODE, S4 = 2, False
PARTS = 4
FT = 2 * TOK
HIDE = -1e30
QUERY, KEY, VALUE = 0, 1, 2
F32, BF16 = jnp.float32, jnp.bfloat16
RING = {0: (0,), 1: (-1, 1), 2: (-2, 2), 3: (-3, 3), 4: (4,)}
Z_UP = (0, -1, 2, -3)


def device(x, y, z, core):
    x, y, z = lax.rem(x + NX, NX), lax.rem(y + NY, NY), lax.rem(z + NZ, NZ)
    return ((x * 4 + lax.div(z, 2)) * 2 + core, lax.rem(z, 2) * NY + y)


def kernel(
    hid, step_in, sizes_in, tmod, cmod, tw, cw, out,
    H, MEAN, RSTD, X, W, T, AKV, AQ, KB, VT, QB, OA, ML, OS, OR, MR, FX, step_ref, sizes_ref,
    loc, hsem, ys, yr, zs, zr, xs, xr, as_, ar, bs, br, os_, or_, fsem,
):
    seq, fsdp = lax.axis_index("seq"), lax.axis_index("fsdp")
    core, zh, x = lax.rem(seq, 2), lax.rem(lax.div(seq, 2), 4), lax.div(seq, 8)
    y, zl = lax.rem(fsdp, NY), lax.div(fsdp, NY)
    z = zh * 2 + zl
    zup, zdown = device(x, y, z + 1, core), device(x, y, z - 1, core)
    zup2, zdown2 = device(x, y, z + 2, core), device(x, y, z - 2, core)
    xup, xdown, xfar = (device(x + k, y, z, core) for k in (1, -1, 2))
    other = device(x, y, z, 1 - core)
    peers = [device(x, y + k, z, core) for k in ((1, -1), (1, -1, 2, -2, 3, -3, 4), (1, -1, 2, -2))[QMODE]]
    peers += [zup, zdown, zup2, zdown2, xup, xdown, xfar, other]

    def shard(par, delta):
        side = zl if par == 0 else 1 - zl
        return side * NY + lax.rem(y + delta + NY, NY)

    own = shard(0, 0)
    started = []

    def send(src, dst, ssem, rsem, to):
        copy = pltpu.make_async_remote_copy(
            src_ref=src, dst_ref=dst, send_sem=ssem, recv_sem=rsem, device_id=to, device_id_type=MESH
        )
        copy.start()
        started.append(copy)

    def arrived(ref, rsem):
        pltpu.make_async_remote_copy(
            src_ref=ref, dst_ref=ref, send_sem=rsem, recv_sem=rsem, device_id=other, device_id_type=MESH
        ).wait_recv()

    take_h = pltpu.make_async_copy(hid.at[0], H.at[pl.ds(0, TOK)], loc.at[0])
    take_h.start()
    take_step = pltpu.make_async_copy(step_in, step_ref, loc.at[3])
    take_step.start()
    take_sizes = pltpu.make_async_copy(sizes_in, sizes_ref, loc.at[4])
    take_sizes.start()

    @pl.when(core == 0)
    def _():
        pltpu.make_async_copy(tw, W.at[own], loc.at[1]).start()
        pltpu.make_async_copy(tmod, T.at[own], loc.at[2]).start()

    @pl.when(core == 1)
    def _():
        pltpu.make_async_copy(cw, W.at[own], loc.at[1]).start()
        pltpu.make_async_copy(cmod, T.at[own], loc.at[2]).start()

    barrier = pltpu.get_barrier_semaphore()
    for peer in peers:
        pl.semaphore_signal(barrier, inc=1, device_id=peer, device_id_type=MESH)
    pltpu.make_async_copy(tw, W.at[own], loc.at[1]).wait()
    pltpu.make_async_copy(tmod, T.at[own], loc.at[2]).wait()
    take_step.wait()
    take_sizes.wait()

    def rows_of(k):
        return pl.ds(pl.multiple_of(lax.rem(x + k + NX, NX) * QR, 16), QR)

    def quarter(d, delta, k=0):
        return W.at[d, pl.ds(0, 3 if S4 and delta == 4 else 1), rows_of(k)]

    def piece(what, d, delta):
        if what == "q":
            return quarter(d, delta)
        if what == "t":
            return T.at[d]
        rows = pl.ds(int(what[1]) * (SH // PARTS), SH // PARTS)
        return W.at[d, KEY if what[0] == "k" else VALUE, rows]

    parts = [kind + str(i) for kind in "kv" for i in range(PARTS)]
    ysems, zsems, xsems = {}, {}, {}

    def ysem(what, delta):
        return ysems.setdefault((what, delta), len(ysems))

    def zsem(what, delta):
        return zsems.setdefault((what, delta), len(zsems))

    def xsem(par, delta, k):
        return xsems.setdefault((par, delta, k), len(xsems))

    def ysend(what, delta, hops):
        there = 4 if abs(delta - hops) == 4 else delta - hops
        i = ysem(what, there)
        ref = piece(what, shard(0, delta), there if what == "q" else delta)
        send(ref, ref, ys.at[i], yr.at[i], device(x, y + hops, z, core))

    def yget(what, delta):
        arrived(piece(what, shard(0, delta), delta), yr.at[ysem(what, delta)])

    def zsend(what, delta):
        if what == "q":
            to = zup if delta in Z_UP else zdown
        else:
            to = zdown if what[0] == "v" else zup
        i = zsem(what, delta)
        ref = piece(what, shard(0, delta), delta)
        send(ref, ref, zs.at[i], zr.at[i], to)

    def zget(what, delta):
        arrived(piece(what, shard(1, delta), delta), zr.at[zsem(what, delta)])

    def xsend(par, delta):
        for k, to in ((1, xup), (-1, xdown), (2, xfar)):
            i = xsem(par, delta, -k if k != 2 else 2)
            ref = quarter(shard(par, delta), delta)
            send(ref, ref, xs.at[i], xr.at[i], to)

    def x_get(par, s):
        for delta in RING[s]:
            for k in (-1, 1, 2):
                arrived(quarter(shard(par, delta), delta, k), xr.at[xsem(par, delta, k)])

    def q_step(s):
        for delta in RING[s]:
            yget("q", delta)
            way = 1 if delta < 0 else -1
            if QMODE == 0 and (s < 3 or delta == -3) or QMODE == 2 and s == 2:
                ysend("q", delta, way)
            if QMODE == 2 and delta == -2:
                ysend("q", delta, 2)
            zsend("q", delta)
            xsend(0, delta)

    def q_cross(s):
        for delta in RING[s]:
            zget("q", delta)
            xsend(1, delta)

    def halfway(what):
        return -1 if what[0] == "v" else 1

    def ring(whats, s):
        for what in whats:
            for delta in RING[s]:
                yget(what, delta)
                way = 1 if delta < 0 else -1
                if s < 3 or (s == 3 and way == halfway(what) and not S4):
                    ysend(what, delta, way)
                zsend(what, delta)

    def cross(whats, s):
        for delta in RING[s]:
            for what in whats:
                zget(what, delta)

    def start_sends():
        for way in (1, -1):
            ysend("t", 0, way)
        for hops in ((1, -1), (4, 1, -1, 2, -2, 3, -3), (2, -2, 1, -1))[QMODE]:
            ysend("q", 0, hops)
        if S4:
            ysend("t", 0, 4)
        zsend("t", 0)
        zsend("q", 0)
        for what in parts:
            for way in (1, -1):
                ysend(what, 0, way)
            zsend(what, 0)

    def norm_rows(first, last):
        def body(i, carry):
            rows = pl.ds(pl.multiple_of(i * 16, 16), 16)
            wide = H[rows, :].astype(F32)
            mean = jnp.sum(wide, axis=1, keepdims=True) * F32(1.0 / D)
            dev = wide - mean
            var = jnp.sum(dev * dev, axis=1, keepdims=True) * F32(1.0 / D)
            MEAN[rows, :] = jnp.broadcast_to(mean, (16, 128))
            RSTD[rows, :] = jnp.broadcast_to(F32(1.0) / jnp.sqrt(var + F32(1e-6)), (16, 128))
            return carry

        lax.fori_loop(first, last, body, 0)

    step = step_ref[0]

    def pair(par, i):
        side = zl if par == 0 else 1 - zl
        turn = 1 - 2 * lax.rem(y, 2)
        k = (0, -turn, turn, 2)[i]
        return side * 4 + lax.rem(lax.div(y, 2) + k + 4, 4)

    def modulate(par, i):
        p = pair(par, i)

        def rows_at(j):
            halves = []
            for h in range(2):
                row = T[2 * p + h, 0, j : j + 1, :]
                for k in range(1, STEPS):
                    row = jnp.where(step == k, T[2 * p + h, k, j : j + 1, :], row)
                halves.append(row)
            return jnp.concatenate(halves, axis=1)

        shift, scale = rows_at(0), F32(1.0) + rows_at(1)
        for r in range(0, FT, 64):
            rows = pl.ds(r, 64)
            wide = H[rows, pl.ds(pl.multiple_of(p * 2 * SH, 128), 2 * SH)].astype(F32)
            mean = jnp.concatenate([MEAN[rows, :]] * 5, axis=1)
            rstd = jnp.concatenate([RSTD[rows, :]] * 5, axis=1)
            X[p, rows, :] = ((wide - mean) * rstd * scale + shift).astype(BF16)

    def slab(p, j):
        return W[pl.ds(2 * p, 2), j].reshape(2 * SH, HD)

    def project(par, i):
        p = pair(par, i)
        w = jnp.concatenate([slab(p, KEY), slab(p, VALUE)], axis=1)
        AKV[...] += jnp.dot(X[p], w, preferred_element_type=F32)

    def query(par, i):
        p = pair(par, i)
        AQ[...] += jnp.dot(X[p], slab(p, QUERY), preferred_element_type=F32)

    def queries(par):
        if par == 1:
            x_get(par, 0)
        for i in range(4):
            x_get(par, i + 1)
            query(par, i)

    def send_kv():
        KB[0] = AKV[:, :HD].astype(BF16)
        send(KB.at[0], KB.at[3], as_.at[0], ar.at[0], zup2)
        send(KB.at[0], KB.at[1], as_.at[1], ar.at[1], zdown2)
        VT[0] = AKV[:, HD:].T.astype(BF16)
        send(VT.at[0], VT.at[3], as_.at[2], ar.at[2], zup2)
        send(VT.at[0], VT.at[1], as_.at[3], ar.at[3], zdown2)

    def send_q():
        QB[0] = AQ[...].astype(BF16)
        send(QB.at[0], QB.at[2], bs.at[1], br.at[1], xfar)
        send(QB.at[0], QB.at[3], bs.at[0], br.at[0], xup)
        send(QB.at[0], QB.at[1], bs.at[2], br.at[2], xdown)

    pl.semaphore_wait(barrier, len(peers))
    start_sends()
    send(hid.at[0], H.at[pl.ds(TOK, TOK)], hsem.at[0], hsem.at[1], other)
    take_h.wait()
    norm_rows(0, 8)
    AKV[...] = jnp.zeros_like(AKV)
    AQ[...] = jnp.zeros_like(AQ)
    ring(("t",),1)
    q_step(1)
    q_step(2)
    arrived(H.at[pl.ds(TOK, TOK)], hsem.at[1])
    norm_rows(8, 16)
    ring(parts,1)
    ring(("t",),2)
    q_cross(0)
    q_step(3)
    q_step(4)
    q_cross(1)
    q_cross(2)
    modulate(0, 0)
    ring(parts,2)
    ring(("t",),3)
    q_cross(3)
    q_cross(4)
    project(0, 0)
    modulate(0, 1)
    ring(parts,3)
    ring(("t",),4)
    cross(("t",),0)
    cross(("t",),1)
    project(0, 1)
    modulate(0, 2)
    modulate(0, 3)
    cross(parts,0)
    modulate(1, 0)
    ring(parts,4)
    project(0, 2)
    cross(parts,1)
    project(1, 0)
    project(0, 3)
    cross(("t",),2)
    cross(("t",),3)
    cross(("t",),4)
    modulate(1, 1)
    modulate(1, 2)
    modulate(1, 3)
    cross(parts,2)
    project(1, 1)
    cross(parts,3)
    project(1, 2)
    cross(parts,4)
    project(1, 3)
    send_kv()
    queries(0)
    queries(1)
    send_q()
    ends = []
    total = jnp.int32(0)
    for j in range(BLKS):
        total = total + sizes_ref[0, j]
        ends.append(total)

    def block_of(frame):
        number = jnp.int32(0)
        for end in ends:
            number = number + jnp.where(end <= frame, jnp.int32(1), jnp.int32(0))
        return number

    root = F32(1.0 / 128.0**0.5)

    def attend(r, slot, first):
        key_block = block_of(x * 4 + lax.rem(zh + slot, 4))
        query_block = block_of(lax.rem(x + r, NX) * 4 + zh)
        bias = jnp.where(key_block <= query_block, F32(0.0), F32(HIDE))
        s = lax.dot_general(KB[slot], QB[r], (((1,), (1,)), ((), ())), preferred_element_type=F32)
        s = s * root + bias
        top = jnp.max(s, axis=0, keepdims=True)
        if not first:
            before = ML[r, 0:1, :]
            top = jnp.maximum(top, before)
            keep = jnp.exp(before - top)
        e = jnp.exp(s - top)
        den = jnp.sum(e, axis=0, keepdims=True)
        o = jnp.dot(VT[slot], e.astype(BF16), preferred_element_type=F32)
        if not first:
            den = den + keep * ML[r, 1:2, :]
            o = o + keep * OA[r]
        ML[r, 0:1, :] = top
        ML[r, 1:2, :] = den
        OA[r] = o

    def attend_planes(slot, first=False):
        for r in range(4):
            attend(r, slot, first)

    arrived(KB.at[3], ar.at[0])
    send(KB.at[3], KB.at[2], as_.at[4], ar.at[4], zup2)
    arrived(KB.at[1], ar.at[1])
    arrived(VT.at[3], ar.at[2])
    arrived(VT.at[1], ar.at[3])
    send(VT.at[1], VT.at[2], as_.at[5], ar.at[5], zdown2)
    for r in (1, 2, 3):
        arrived(QB.at[r], br.at[3 - r])
    attend_planes(0, first=True)
    attend_planes(1)
    attend_planes(3)
    arrived(KB.at[2], ar.at[4])
    arrived(VT.at[2], ar.at[5])

    for r, to in ((2, xfar), (1, xup), (3, xdown)):
        attend(r, 2, False)
        OS[r - 1] = OA[r].astype(BF16)
        send(OS.at[r - 1], OR.at[3 - r], os_.at[r - 1], or_.at[r - 1], to)
        send(ML.at[r], MR.at[3 - r], os_.at[r + 2], or_.at[r + 2], to)
    attend(0, 2, False)
    for r in (2, 1, 3):
        arrived(OR.at[3 - r], or_.at[r - 1])
        arrived(MR.at[3 - r], or_.at[r + 2])
    top = ML[0, 0:1, :]
    for i in range(3):
        top = jnp.maximum(top, MR[i, 0:1, :])
    w = jnp.exp(ML[0, 0:1, :] - top)
    den, o = w * ML[0, 1:2, :], w * OA[0]
    for i in range(3):
        w = jnp.exp(MR[i, 0:1, :] - top)
        den = den + w * MR[i, 1:2, :]
        o = o + w * OR[i].astype(F32)
    o = (o / den).T
    FX[0] = o[TOK:, :]
    send(FX.at[0], FX.at[1], fsem.at[0], fsem.at[1], other)
    arrived(FX.at[1], fsem.at[1])
    sign = jnp.where(core == 0, F32(1.0), F32(-1.0))
    out[0] = (FX[1] - o[:TOK, :]) * sign

    for copy in started:
        copy.wait_send()


def per_device(hidden, step_index, block_sizes, teacher_mod, critic_mod, teacher_weights, critic_weights):
    vmem, hbm = (pl.BlockSpec(memory_space=m) for m in (pltpu.VMEM, pltpu.HBM))
    dma = pltpu.SemaphoreType.DMA
    return pl.pallas_call(
        kernel,
        out_shape=jax.ShapeDtypeStruct((1, TOK, HD), F32),
        in_specs=[hbm] * 7,
        out_specs=vmem,
        scratch_shapes=[
            pltpu.VMEM((FT, D), BF16),
            pltpu.VMEM((FT, 128), F32),
            pltpu.VMEM((FT, 128), F32),
            pltpu.VMEM((8, FT, 2 * SH), BF16),
            pltpu.VMEM((16, 3, SH, HD), BF16),
            pltpu.VMEM((16, STEPS, 2, SH), F32),
            pltpu.VMEM((FT, 2 * HD), F32),
            pltpu.VMEM((FT, HD), F32),
            pltpu.VMEM((4, FT, HD), BF16),
            pltpu.VMEM((4, HD, FT), BF16),
            pltpu.VMEM((4, FT, HD), BF16),
            pltpu.VMEM((4, HD, FT), F32),
            pltpu.VMEM((4, 8, FT), F32),
            pltpu.VMEM((3, HD, FT), BF16),
            pltpu.VMEM((3, HD, FT), BF16),
            pltpu.VMEM((3, 8, FT), F32),
            pltpu.VMEM((2, TOK, HD), F32),
            pltpu.SMEM((1,), jnp.int32),
            pltpu.SMEM((1, BLKS), jnp.int32),
            dma((5,)),
            dma((2,)),
            dma((72,)),
            dma((72,)),
            dma((80,)),
            dma((80,)),
            dma((45,)),
            dma((45,)),
            dma((6,)),
            dma((6,)),
            dma((3,)),
            dma((3,)),
            dma((6,)),
            dma((6,)),
            dma((2,)),
        ],
        compiler_params=pltpu.CompilerParams(
            collective_id=0, has_side_effects=True, vmem_limit_bytes=63 * 2**20
        ),
        cost_estimate=pl.CostEstimate(flops=3 * 10**9, bytes_accessed=4 * 10**6, transcendentals=10**6),
    )(hidden, step_index, block_sizes, teacher_mod, critic_mod, teacher_weights, critic_weights)


def solution(mesh):
    return jax.shard_map(
        per_device,
        mesh=mesh,
        in_specs=(
            P("fsdp", "seq", None),
            P("fsdp"),
            P("fsdp", None),
            P(None, None, "fsdp"),
            P(None, None, "fsdp"),
            P(None, "fsdp", None),
            P(None, "fsdp", None),
        ),
        out_specs=P("fsdp", "seq", None),
        check_vma=False,
    )
```

```python
import jax
import jax.numpy as jnp
from jax import lax
from jax.experimental import pallas as pl
from jax.experimental.pallas import tpu as pltpu
from jax.sharding import PartitionSpec as P

MESH = pl.DeviceIdType.MESH
NX, NY, NZ = 4, 8, 8
D, HD, TOK = 5120, 128, 128
SH = D // 16
QR = SH // NX
STEPS, BLKS = 4, 6
QMODE, S4, SPLIT = 2, False, False
PARTS = 4
FT = 2 * TOK
HIDE = -1e30
QUERY, KEY, VALUE = 0, 1, 2
F32, BF16 = jnp.float32, jnp.bfloat16
RING = {0: (0,), 1: (-1, 1), 2: (-2, 2), 3: (-3, 3), 4: (4,)}
Z_UP = (0, -1, 2, -3)


def device(x, y, z, core):
    x, y, z = lax.rem(x + NX, NX), lax.rem(y + NY, NY), lax.rem(z + NZ, NZ)
    return ((x * 4 + lax.div(z, 2)) * 2 + core, lax.rem(z, 2) * NY + y)


def kernel(
    hid, step_in, sizes_in, tmod, cmod, tw, cw, out,
    H, MEAN, RSTD, X, W, T, AKV, AQ, KB, VT, QB, OA, ML, OS, OR, MR, OF, step_ref, sizes_ref,
    loc, hsem, ys, yr, zs, zr, xs, xr, as_, ar, bs, br, os_, or_, ms, mr,
):
    seq, fsdp = lax.axis_index("seq"), lax.axis_index("fsdp")
    core, zh, x = lax.rem(seq, 2), lax.rem(lax.div(seq, 2), 4), lax.div(seq, 8)
    y, zl = lax.rem(fsdp, NY), lax.div(fsdp, NY)
    z = zh * 2 + zl
    zup, zdown = device(x, y, z + 1, core), device(x, y, z - 1, core)
    along_x = core if SPLIT else 0 * core
    along_z = 1 - along_x
    kup, kdown = (device(x + k * along_x, y, z + 2 * k * along_z, core) for k in (1, -1))
    qup, qdown, qfar = (
        [device(x + k * along_z, y, z + 2 * k * along_x, c) for c in (core, 1 - core)] for k in (1, -1, 2)
    )
    xup, xdown, xfar = (device(x + k, y, z, core) for k in (1, -1, 2))
    other = device(x, y, z, 1 - core)
    peers = [device(x, y + k, z, core) for k in ((1, -1), (1, -1, 2, -2, 3, -3, 4), (1, -1, 2, -2), (1, -1, 2, -2, 4))[QMODE]]
    peers += [device(x, y, z + k, core) for k in (2, -2)] + [zup, zdown, xup, xdown, xfar, other, qup[1], qdown[1], qfar[1]]

    def shard(par, delta):
        side = zl if par == 0 else 1 - zl
        return side * NY + lax.rem(y + delta + NY, NY)

    own = shard(0, 0)
    started = []

    def send(src, dst, ssem, rsem, to):
        copy = pltpu.make_async_remote_copy(
            src_ref=src, dst_ref=dst, send_sem=ssem, recv_sem=rsem, device_id=to, device_id_type=MESH
        )
        copy.start()
        started.append(copy)

    def arrived(ref, rsem):
        pltpu.make_async_remote_copy(
            src_ref=ref, dst_ref=ref, send_sem=rsem, recv_sem=rsem, device_id=other, device_id_type=MESH
        ).wait_recv()

    take_h = pltpu.make_async_copy(hid.at[0], H.at[pl.ds(0, TOK)], loc.at[0])
    take_h.start()
    take_step = pltpu.make_async_copy(step_in, step_ref, loc.at[3])
    take_step.start()
    take_sizes = pltpu.make_async_copy(sizes_in, sizes_ref, loc.at[4])
    take_sizes.start()

    @pl.when(core == 0)
    def _():
        pltpu.make_async_copy(tw, W.at[own], loc.at[1]).start()
        pltpu.make_async_copy(tmod, T.at[own], loc.at[2]).start()

    @pl.when(core == 1)
    def _():
        pltpu.make_async_copy(cw, W.at[own], loc.at[1]).start()
        pltpu.make_async_copy(cmod, T.at[own], loc.at[2]).start()

    barrier = pltpu.get_barrier_semaphore()
    for peer in peers:
        pl.semaphore_signal(barrier, inc=1, device_id=peer, device_id_type=MESH)
    pltpu.make_async_copy(tw, W.at[own], loc.at[1]).wait()
    pltpu.make_async_copy(tmod, T.at[own], loc.at[2]).wait()
    take_step.wait()
    take_sizes.wait()

    def rows_of(k):
        return pl.ds(pl.multiple_of(lax.rem(x + k + NX, NX) * QR, 16), QR)

    def quarter(d, delta, k=0):
        return W.at[d, pl.ds(0, 3 if S4 and delta == 4 else 1), rows_of(k)]

    def piece(what, d, delta):
        if what == "q":
            return quarter(d, delta)
        if what == "t":
            return T.at[d]
        rows = pl.ds(int(what[1]) * (SH // PARTS), SH // PARTS)
        return W.at[d, KEY if what[0] == "k" else VALUE, rows]

    parts = [kind + str(i) for kind in "kv" for i in range(PARTS)]
    ysems, zsems, xsems = {}, {}, {}

    def ysem(what, delta):
        return ysems.setdefault((what, delta), len(ysems))

    def zsem(what, delta):
        return zsems.setdefault((what, delta), len(zsems))

    def xsem(par, delta, k):
        return xsems.setdefault((par, delta, k), len(xsems))

    def ysend(what, delta, hops):
        there = 4 if abs(delta - hops) == 4 else delta - hops
        i = ysem(what, there)
        ref = piece(what, shard(0, delta), there if what == "q" else delta)
        send(ref, ref, ys.at[i], yr.at[i], device(x, y + hops, z, core))

    def yget(what, delta):
        arrived(piece(what, shard(0, delta), delta), yr.at[ysem(what, delta)])

    def zsend(what, delta):
        if what == "q":
            to = zup if delta in Z_UP else zdown
        else:
            to = zdown if what[0] == "v" else zup
        i = zsem(what, delta)
        ref = piece(what, shard(0, delta), delta)
        send(ref, ref, zs.at[i], zr.at[i], to)

    def zget(what, delta):
        arrived(piece(what, shard(1, delta), delta), zr.at[zsem(what, delta)])

    def xsend(par, delta):
        for k, to in ((1, xup), (-1, xdown), (2, xfar)):
            i = xsem(par, delta, -k if k != 2 else 2)
            ref = quarter(shard(par, delta), delta)
            send(ref, ref, xs.at[i], xr.at[i], to)

    def x_get(par, s):
        for delta in RING[s]:
            for k in (-1, 1, 2):
                arrived(quarter(shard(par, delta), delta, k), xr.at[xsem(par, delta, k)])

    def q_step(s):
        for delta in RING[s]:
            yget("q", delta)
            way = 1 if delta < 0 else -1
            if QMODE == 0 and (s < 3 or delta == -3) or QMODE >= 2 and s == 2:
                ysend("q", delta, way)
            if QMODE == 2 and delta == -2:
                ysend("q", delta, 2)
            zsend("q", delta)
            xsend(0, delta)

    def q_cross(s):
        for delta in RING[s]:
            zget("q", delta)
            xsend(1, delta)

    def halfway(what):
        return -1 if what[0] == "v" else 1

    def ring(whats, s):
        for what in whats:
            for delta in RING[s]:
                yget(what, delta)
                way = 1 if delta < 0 else -1
                if s < 3 or (s == 3 and way == halfway(what) and not S4):
                    ysend(what, delta, way)
                zsend(what, delta)

    def cross(whats, s):
        for delta in RING[s]:
            for what in whats:
                zget(what, delta)

    def start_sends():
        for way in (1, -1):
            ysend("t", 0, way)
        for hops in ((1, -1), (4, 1, -1, 2, -2, 3, -3), (2, -2, 1, -1), (4, 1, -1, 2, -2))[QMODE]:
            ysend("q", 0, hops)
        if S4:
            ysend("t", 0, 4)
        zsend("t", 0)
        zsend("q", 0)
        for what in parts:
            for way in (1, -1):
                ysend(what, 0, way)
            zsend(what, 0)

    def norm_rows(first, last):
        def body(i, carry):
            rows = pl.ds(pl.multiple_of(i * 16, 16), 16)
            wide = H[rows, :].astype(F32)
            mean = jnp.sum(wide, axis=1, keepdims=True) * F32(1.0 / D)
            dev = wide - mean
            var = jnp.sum(dev * dev, axis=1, keepdims=True) * F32(1.0 / D)
            MEAN[rows, :] = jnp.broadcast_to(mean, (16, 128))
            RSTD[rows, :] = jnp.broadcast_to(F32(1.0) / jnp.sqrt(var + F32(1e-6)), (16, 128))
            return carry

        lax.fori_loop(first, last, body, 0)

    step = step_ref[0]

    def pair(par, i):
        side = zl if par == 0 else 1 - zl
        turn = 1 - 2 * lax.rem(y, 2)
        k = (0, -turn, turn, 2)[i]
        return side * 4 + lax.rem(lax.div(y, 2) + k + 4, 4)

    def modulate(par, i):
        p = pair(par, i)

        def rows_at(j):
            halves = []
            for h in range(2):
                row = T[2 * p + h, 0, j : j + 1, :]
                for k in range(1, STEPS):
                    row = jnp.where(step == k, T[2 * p + h, k, j : j + 1, :], row)
                halves.append(row)
            return jnp.concatenate(halves, axis=1)

        shift, scale = rows_at(0), F32(1.0) + rows_at(1)
        for r in range(0, FT, 64):
            rows = pl.ds(r, 64)
            wide = H[rows, pl.ds(pl.multiple_of(p * 2 * SH, 128), 2 * SH)].astype(F32)
            mean = jnp.concatenate([MEAN[rows, :]] * 5, axis=1)
            rstd = jnp.concatenate([RSTD[rows, :]] * 5, axis=1)
            X[p, rows, :] = ((wide - mean) * rstd * scale + shift).astype(BF16)

    def slab(p, j):
        return W[pl.ds(2 * p, 2), j].reshape(2 * SH, HD)

    def project(par, i):
        p = pair(par, i)
        w = jnp.concatenate([slab(p, KEY), slab(p, VALUE)], axis=1)
        AKV[...] += jnp.dot(X[p], w, preferred_element_type=F32)

    def query(par, i):
        p = pair(par, i)
        AQ[...] += jnp.dot(X[p], slab(p, QUERY), preferred_element_type=F32)

    def queries(par):
        if par == 1:
            x_get(par, 0)
        for i in range(4):
            if i < 3 or not S4:
                x_get(par, i + 1)
            query(par, i)

    def send_k():
        KB[0] = AKV[:, :HD].astype(BF16)
        send(KB.at[0], KB.at[3], as_.at[0], ar.at[0], kup)
        send(KB.at[0], KB.at[1], as_.at[1], ar.at[1], kdown)

    def send_v():
        VT[0] = AKV[:, HD:].T.astype(BF16)
        send(VT.at[0], VT.at[3], as_.at[2], ar.at[2], kup)
        send(VT.at[0], VT.at[1], as_.at[3], ar.at[3], kdown)

    def send_q():
        QB[0] = AQ[...].astype(BF16)
        send(QB.at[0], QB.at[2], bs.at[1], br.at[1], qfar[0])
        send(QB.at[0], QB.at[3], bs.at[0], br.at[0], qup[0])
        send(QB.at[0], QB.at[1], bs.at[2], br.at[2], qdown[0])

    pl.semaphore_wait(barrier, len(peers))
    start_sends()
    send(hid.at[0], H.at[pl.ds(TOK, TOK)], hsem.at[0], hsem.at[1], other)
    take_h.wait()
    norm_rows(0, 8)
    AKV[...] = jnp.zeros_like(AKV)
    AQ[...] = jnp.zeros_like(AQ)
    ring(("t",),1)
    q_step(1)
    q_step(2)
    arrived(H.at[pl.ds(TOK, TOK)], hsem.at[1])
    norm_rows(8, 16)
    ring(parts,1)
    ring(("t",),2)
    q_cross(0)
    q_step(3)
    q_step(4)
    q_cross(1)
    q_cross(2)
    modulate(0, 0)
    ring(parts,2)
    ring(("t",),3)
    q_cross(3)
    q_cross(4)
    project(0, 0)
    modulate(0, 1)
    ring(parts,3)
    ring(("t",),4)
    cross(("t",),0)
    cross(("t",),1)
    project(0, 1)
    modulate(0, 2)
    modulate(0, 3)
    cross(parts,0)
    modulate(1, 0)
    ring(parts,4)
    project(0, 2)
    cross(parts,1)
    project(1, 0)
    project(0, 3)
    cross(("t",),2)
    cross(("t",),3)
    cross(("t",),4)
    modulate(1, 1)
    modulate(1, 2)
    modulate(1, 3)
    cross(parts,2)
    project(1, 1)
    cross(parts,3)
    project(1, 2)
    cross(parts,4)
    project(1, 3)
    send_k()
    send_v()
    queries(0)
    queries(1)
    send_q()
    ends = []
    total = jnp.int32(0)
    for j in range(BLKS):
        total = total + sizes_ref[0, j]
        ends.append(total)

    def block_of(frame):
        number = jnp.int32(0)
        for end in ends:
            number = number + jnp.where(end <= frame, jnp.int32(1), jnp.int32(0))
        return number

    root = F32(1.0 / 128.0**0.5)

    def attend(r, slot, first):
        key_block = block_of(lax.rem(x + along_x * slot, 4) * 4 + lax.rem(zh + along_z * slot, 4))
        query_block = block_of(lax.rem(x + along_z * r, 4) * 4 + lax.rem(zh + along_x * r, 4))
        bias = jnp.where(key_block <= query_block, F32(0.0), F32(HIDE))
        s = lax.dot_general(KB[slot], QB[r], (((1,), (1,)), ((), ())), preferred_element_type=F32)
        s = s * root + bias
        top = jnp.max(s, axis=0, keepdims=True)
        if not first:
            before = ML[r, 0:1, :]
            top = jnp.maximum(top, before)
            keep = jnp.exp(before - top)
        e = jnp.exp(s - top)
        den = jnp.sum(e, axis=0, keepdims=True)
        o = jnp.dot(VT[slot], e.astype(BF16), preferred_element_type=F32)
        if not first:
            den = den + keep * ML[r, 1:2, :]
            o = o + keep * OA[r]
        ML[r, 0:1, :] = top
        ML[r, 1:2, :] = den
        OA[r] = o

    def attend_planes(slot, first=False):
        for r in range(4):
            attend(r, slot, first)

    arrived(KB.at[3], ar.at[0])
    send(KB.at[3], KB.at[2], as_.at[4], ar.at[4], kup)
    arrived(KB.at[1], ar.at[1])
    arrived(VT.at[3], ar.at[2])
    arrived(VT.at[1], ar.at[3])
    send(VT.at[1], VT.at[2], as_.at[5], ar.at[5], kdown)
    for r in (1, 2, 3):
        arrived(QB.at[r], br.at[3 - r])
    attend_planes(0, first=True)
    attend_planes(1)
    attend_planes(3)
    arrived(KB.at[2], ar.at[4])
    arrived(VT.at[2], ar.at[5])

    def give(r, h, o_ref, to):
        i, j = h * 4 + (4 - r) % 4, h * 4 + r
        send(o_ref, OR.at[h, (4 - r) % 4] if r else OF, os_.at[j], or_.at[i], to)
        send(ML.at[r, :, pl.ds(h * TOK, TOK)], MR.at[h, (4 - r) % 4], ms.at[j], mr.at[i], to)

    def got(r, h):
        arrived(OR.at[h, r] if r else OF, or_.at[h * 4 + r])
        arrived(MR.at[h, r], mr.at[h * 4 + r])

    for r, to in ((2, qfar), (1, qup), (3, qdown)):
        attend(r, 2, False)
        for h in range(2):
            OS[r, h] = OA[r, :, h * TOK : (h + 1) * TOK].astype(BF16)
            give(r, h, OS.at[r, h], to[h])
    attend(0, 2, False)
    give(0, 1, OA.at[0, :, pl.ds(TOK, TOK)], other)

    def combine(h):
        own = ML[0, :, :TOK] if h == 0 else MR[1, 0]
        parts_ = [own] + [MR[h, r] for r in (1, 2, 3)]
        top = parts_[0][0:1, :]
        for part in parts_[1:]:
            top = jnp.maximum(top, part[0:1, :])
        den, o = F32(0.0), F32(0.0)
        for r, part in enumerate(parts_):
            w = jnp.exp(part[0:1, :] - top)
            den = den + w * part[1:2, :]
            if r == 0:
                o = o + w * (OA[0, :, :TOK] if h == 0 else OF[...])
            else:
                o = o + w * OR[h, r].astype(F32)
        return o / den

    got(0, 1)
    for r in (1, 3, 2):
        for h in range(2):
            got(r, h)
    sign = jnp.where(core == 0, F32(1.0), F32(-1.0))
    out[0] = ((combine(1) - combine(0)) * sign).T

    for copy in started:
        copy.wait_send()


def per_device(hidden, step_index, block_sizes, teacher_mod, critic_mod, teacher_weights, critic_weights):
    vmem, hbm = (pl.BlockSpec(memory_space=m) for m in (pltpu.VMEM, pltpu.HBM))
    dma = pltpu.SemaphoreType.DMA
    return pl.pallas_call(
        kernel,
        out_shape=jax.ShapeDtypeStruct((1, TOK, HD), F32),
        in_specs=[hbm] * 7,
        out_specs=vmem,
        scratch_shapes=[
            pltpu.VMEM((FT, D), BF16),
            pltpu.VMEM((FT, 128), F32),
            pltpu.VMEM((FT, 128), F32),
            pltpu.VMEM((8, FT, 2 * SH), BF16),
            pltpu.VMEM((16, 3, SH, HD), BF16),
            pltpu.VMEM((16, STEPS, 2, SH), F32),
            pltpu.VMEM((FT, 2 * HD), F32),
            pltpu.VMEM((FT, HD), F32),
            pltpu.VMEM((4, FT, HD), BF16),
            pltpu.VMEM((4, HD, FT), BF16),
            pltpu.VMEM((4, FT, HD), BF16),
            pltpu.VMEM((4, HD, FT), F32),
            pltpu.VMEM((4, 8, FT), F32),
            pltpu.VMEM((4, 2, HD, TOK), BF16),
            pltpu.VMEM((2, 4, HD, TOK), BF16),
            pltpu.VMEM((2, 4, 8, TOK), F32),
            pltpu.VMEM((HD, TOK), F32),
            pltpu.SMEM((1,), jnp.int32),
            pltpu.SMEM((1, BLKS), jnp.int32),
            dma((5,)),
            dma((2,)),
            dma((72,)),
            dma((72,)),
            dma((80,)),
            dma((80,)),
            dma((45,)),
            dma((45,)),
            dma((6,)),
            dma((6,)),
            dma((3,)),
            dma((3,)),
            dma((8,)),
            dma((8,)),
            dma((8,)),
            dma((8,)),
        ],
        compiler_params=pltpu.CompilerParams(
            collective_id=0, has_side_effects=True, vmem_limit_bytes=63 * 2**20
        ),
        cost_estimate=pl.CostEstimate(flops=3 * 10**9, bytes_accessed=4 * 10**6, transcendentals=10**6),
    )(hidden, step_index, block_sizes, teacher_mod, critic_mod, teacher_weights, critic_weights)


def solution(mesh):
    return jax.shard_map(
        per_device,
        mesh=mesh,
        in_specs=(
            P("fsdp", "seq", None),
            P("fsdp"),
            P("fsdp", None),
            P(None, None, "fsdp"),
            P(None, None, "fsdp"),
            P(None, "fsdp", None),
            P(None, "fsdp", None),
        ),
        out_specs=P("fsdp", "seq", None),
        check_vma=False,
    )
```
